256 devices in a mesh: pix: 32 (over x_lo, z, core), mem: 8 (over y, x_hi).
Axes of the slice: x: 4 (x_hi: 2, x_lo: 2; x = x_hi * 2 + x_lo), y: 4, z: 8, core: 2. Of those that a mesh axis runs over, the one named last changes fastest.
Arguments:
- anomalies: bfloat16 [8192, 4096], P('pix', 'mem'), may hold values from -0.17860863 to 0.17860863
- obs_weight: float32 [8192], P('pix'), may hold values from 0.2 to 5
Outputs:
- factored: float32 [4096, 4096], P('pix', 'mem')
The draws below stay inside these ranges and needn't reach their ends.
All inputs are finite; a program needn't handle non-finite values.
Results may differ from the reference program's by a relative error of at most 0.0034.
Values may be sent and summed in bfloat16 or wider, within the bound.
No kernel may reach another device: no remote copies, remote signals or barrier semaphores. Data moves between devices by JAX's collectives and lax.ppermute only.
A program may use at most 128 MiB of HBM per device.

```python
import math
import jax
import jax.numpy as jnp
from jax import lax

M = 4096
NB = 512
PANELS = 2
PIXELS = 8192


def draw_anomalies(key, part):
    key = jax.random.fold_in(key, 11)
    groups = max(M // 128, 4)
    key_group, key_noise, key_field, key_amp = jax.random.split(key, 4)
    member_group = jax.random.randint(key_group, (M,), 0, groups)
    field = jnp.clip(jax.random.normal(key_field, (PIXELS, groups), jnp.float32), -4.0, 4.0)
    shared = jnp.take(field, member_group, axis=1)
    noise = jnp.clip(jax.random.normal(key_noise, (PIXELS, M), jnp.float32), -4.0, 4.0)
    amplitude = jax.random.uniform(key_amp, (M,), jnp.float32, 0.4, 1.0)
    values = (noise + amplitude[None, :] * shared) * (1.5 * M) ** (-0.5)
    return values.astype(jnp.bfloat16)


def block_scale(own_key, shape, cuts, smallest, top_value):
    factor_of = 1.0
    for axis_at, parts in cuts:
        draws = jax.random.uniform(jax.random.fold_in(jax.random.fold_in(own_key, 6), axis_at), (parts,), jnp.float32, smallest / len(cuts), top_value / len(cuts))
        factor_of = factor_of * jnp.repeat(jnp.exp(draws), shape[axis_at] // parts).reshape((-1,) + (1,) * (len(shape) - 1 - axis_at))
    return factor_of


def setup_inputs(seed: int = 0) -> dict:
    key_of = jax.random.split(jax.random.key(seed), 3)
    return {
        "anomalies": draw_anomalies(jax.random.fold_in(key_of[2], 71), 0),
        "obs_weight": jnp.clip(jnp.exp(math.log(5.0) - 3.218876 * jax.random.uniform(key_of[1], (PIXELS,), jnp.float32) ** block_scale(key_of[1], (PIXELS,), ((0, 32),), -0.2, 0.2)), 0.2, 5.0),
    }


def reference(anomalies, obs_weight):
    weighted = (anomalies.astype(jnp.float32) * jnp.sqrt(obs_weight)[:, None]).astype(jnp.bfloat16)
    gram = lax.dot_general(weighted.astype(jnp.float32), weighted.astype(jnp.float32), (((0,), (0,)), ((), ())), preferred_element_type=jnp.float32)
    factored = gram + jnp.eye(M, dtype=jnp.float32)
    row_ids = jnp.arange(M, dtype=jnp.int32)
    for panel_step in range(PANELS):
        start = NB * panel_step
        block = factored[start:start + NB, start:start + NB]
        chol = jnp.linalg.cholesky(block)
        panel = factored[:, start:start + NB]
        solved = lax.linalg.triangular_solve(chol, panel, left_side=False, lower=True, transpose_a=True)
        diag_rows = jnp.tril(chol) + jnp.triu(block, 1)
        placed = jnp.concatenate([jnp.zeros((start, NB), jnp.float32), diag_rows, jnp.zeros((M - start - NB, NB), jnp.float32)], axis=0)
        below = (row_ids >= start + NB)[:, None]
        inside = ((row_ids >= start) & (row_ids < start + NB))[:, None]
        new_panel = jnp.where(below, solved, jnp.where(inside, placed, panel))
        lower = jnp.where(below, solved, jnp.zeros_like(solved)).astype(jnp.bfloat16)
        update = jnp.dot(lower.astype(jnp.float32), lower.T.astype(jnp.float32), preferred_element_type=jnp.float32)
        factored = lax.dynamic_update_slice(factored, new_panel, (0, start))
        factored = factored - update
    return factored
```

```python
import jax
import jax.numpy as jnp
from jax import lax
from jax.experimental import pallas as pl
from jax.experimental.pallas import tpu as pltpu
from jax.sharding import Mesh, PartitionSpec as P

NB = 512
B = 128
PIX = ("xlo", "z", "core")
MEM = ("y", "xhi")
SIZES = {"xlo": 2, "z": 8, "core": 2, "y": 4, "xhi": 2}
F32 = jnp.float32
BF16 = jnp.bfloat16


def dot(a, b, ca, cb):
    dims = (((ca,), (cb,)), ((), ()))
    return lax.dot_general(a, b, dims, precision=lax.Precision.HIGHEST, preferred_element_type=F32)


def factor_block(a_ref, w_ref, o):
    n = B // 8
    A = [a_ref[o + 8 * i : o + 8 * i + 8, o : o + B] for i in range(n)]
    lane = lax.broadcasted_iota(jnp.int32, (8, B), 1)
    sub = lax.broadcasted_iota(jnp.int32, (8, B), 0)
    E = [jnp.where(lane == sub + 8 * i, 1.0, 0.0).astype(F32) for i in range(n)]
    for b in range(n):
        lo = 8 * b
        R, G = A[b], E[b]
        s = {}
        for k in range(8):
            for i in range(k, 8):
                s[i, k] = jnp.broadcast_to(R[k : k + 1, lo + i : lo + i + 1], (1, B))
        inv, l = [None] * 8, {}
        for k in range(8):
            inv[k] = 1.0 / s[k, k]
            for i in range(k + 1, 8):
                l[i, k] = s[i, k] * inv[k]
            for j in range(k + 1, 8):
                for i in range(j, 8):
                    s[i, j] = s[i, j] - s[i, k] * l[j, k]
        r = [R[k : k + 1, :] for k in range(8)]
        f = [G[k : k + 1, :] for k in range(8)]
        for k in range(8):
            for i in range(k + 1, 8):
                r[i] = r[i] - l[i, k] * r[k]
                f[i] = f[i] - l[i, k] * f[k]
        for k in range(8):
            w_ref[lo + k : lo + k + 1, :] = f[k] * lax.rsqrt(s[k, k])
        if b == n - 1:
            break
        v = [r[k] * inv[k] for k in range(8)]
        g = [f[k] * inv[k] for k in range(8)]
        for k in range(7, -1, -1):
            for i in range(k):
                v[i] = v[i] - l[k, i] * v[k]
                g[i] = g[i] - l[k, i] * g[k]
        for i in range(b + 1, n):
            c = [jnp.broadcast_to(A[i][:, lo + k : lo + k + 1], (8, B)) for k in range(8)]
            acc, ace = c[0] * v[0], c[0] * g[0]
            for k in range(1, 8):
                acc = acc + c[k] * v[k]
                ace = ace + c[k] * g[k]
            A[i] = A[i] - acc
            E[i] = E[i] - ace


def inverse_factor_kernel(a_in, out_ref, a_ref, e_ref, w_ref):
    N = a_in.shape[0]
    n = N // B
    a_ref[...] = a_in[...]
    e_ref[...] = jnp.zeros((N, N), F32)
    out_ref[...] = jnp.zeros((N, N), F32)
    for k in range(n):
        o = k * B
        factor_block(a_ref, w_ref, o)
        W = w_ref[...]
        out_ref[o : o + B, o : o + B] = W
        if k > 0:
            out_ref[o : o + B, :o] = dot(W, e_ref[o : o + B, :o], 1, 0)
        if k < n - 1:
            U = dot(W, a_ref[o : o + B, o + B :], 1, 0)
            a_ref[o + B :, o + B :] = a_ref[o + B :, o + B :] - dot(U, U, 0, 0)
            e_ref[o + B :, : o + B] = e_ref[o + B :, : o + B] - dot(U, out_ref[o : o + B, : o + B], 0, 0)


def inverse_factor(a):
    N = a.shape[0]
    return pl.pallas_call(
        inverse_factor_kernel,
        out_shape=jax.ShapeDtypeStruct((N, N), F32),
        in_specs=[pl.BlockSpec(memory_space=pltpu.VMEM)],
        out_specs=pl.BlockSpec(memory_space=pltpu.VMEM),
        scratch_shapes=[pltpu.VMEM((N, N), F32), pltpu.VMEM((N, N), F32), pltpu.VMEM((B, B), F32)],
        compiler_params=pltpu.CompilerParams(vmem_limit_bytes=24 << 20),
        cost_estimate=pl.CostEstimate(flops=10**10, bytes_accessed=64 << 20, transcendentals=0),
    )(a)


def shift(x, axis, d):
    n = SIZES[axis]
    return lax.ppermute(x, axis, [(i, (i + d) % n) for i in range(n)])


def flip(x, axis):
    n = SIZES[axis]
    return lax.ppermute(x, axis, [(i, i ^ 1) for i in range(n)])


def both(x, axis):
    o = flip(x, axis)
    first = lax.axis_index(axis) % 2 == 0
    return jnp.stack([jnp.where(first, x, o), jnp.where(first, o, x)])


def take(x, i):
    return lax.dynamic_index_in_dim(x, i, 0, keepdims=False)


def ring_y(x):
    y = lax.axis_index("y")
    below, above = shift(x, "y", 1), shift(x, "y", -1)
    far = jnp.stack([shift(below[0], "y", 1), shift(above[1], "y", -1)])
    out = jnp.zeros((4,) + x.shape, x.dtype)
    for d, part in ((0, x), (3, below), (1, above), (2, far)):
        out = lax.dynamic_update_index_in_dim(out, part, (y + d) % 4, 0)
    return out


def from_y0(x):
    y = lax.axis_index("y")
    up = lax.ppermute(x, "y", [(0, 1)])
    down = lax.ppermute(x, "y", [(0, 3)])
    x = jnp.where(y == 1, up, jnp.where(y == 3, down, x))
    a = lax.ppermute(x[0], "y", [(1, 2)])
    b = lax.ppermute(x[1], "y", [(3, 2)])
    return jnp.where(y == 2, jnp.stack([a, b]), x)


def from_member0(x):
    c = lax.axis_index("core")
    half = take(x.reshape((2, 2, NB // 4) + x.shape[1:]), c)
    o = lax.ppermute(half, "xhi", [(0, 1)])
    half = jnp.where(lax.axis_index("xhi") == 0, half, o)
    half = from_y0(half)
    return both(half, "core").reshape(x.shape)


def mm(a, b, ca=1, cb=0, precision=lax.Precision.HIGH):
    return lax.dot_general(a, b, (((ca,), (cb,)), ((), ())), precision=precision, preferred_element_type=F32)


def local(anomalies, obs_weight):
    xl, z, c, y, xh = (lax.axis_index(a) for a in PIX + MEM)
    b, q = z % 2, z // 2
    m = 2 * y + xh
    p = (xl * 8 + z) * 2 + c
    w = (anomalies.astype(F32) * jnp.sqrt(obs_weight)[:, None]).astype(BF16)

    pair = jnp.concatenate([w, flip(w, "z")], axis=0)
    rows = lax.dynamic_slice_in_dim(pair, b * 256, 256, 1)
    rows = ring_y(both(rows, "xhi")).reshape(8, 512, 256)

    def partial(core):
        r = lax.dynamic_slice_in_dim(rows, core * B, B, 2)
        return lax.dot_general(r, pair, (((1,), (0,)), ((), ())), preferred_element_type=F32)

    given = flip(partial(1 - c), "core")
    part = partial(c) + given

    top = part[:2]
    u = take(top, xl) + flip(take(top, 1 - xl), "xlo")
    u = u.reshape(4, 32, NB)
    v = take(u, q)
    for d in range(1, 4):
        v = v + shift(take(u, (q + d) % 4), "z", 2 * d)
    t = jnp.zeros((8, 32, NB), F32)
    t = lax.dynamic_update_index_in_dim(t, v, z, 0)
    for d in range(1, 8):
        t = lax.dynamic_update_index_in_dim(t, shift(v, "z", d), (z + 8 - d) % 8, 0)
    t = both(both(t, "xlo"), "core")
    t = t.reshape(2, 2, 4, 2, 32, NB).transpose(1, 3, 0, 2, 4, 5).reshape(2, NB, NB)
    eye = jnp.eye(NB, dtype=F32)
    t0 = t[0] + jnp.where(m == 0, eye, 0)
    t1 = t[1] + jnp.where(m == 1, eye, 0)

    part = part.reshape(2, 4, B, NB)
    e = take(part, xl) + flip(take(part, 1 - xl).astype(BF16), "xlo").astype(F32)
    tile = take(e, q)
    for d in range(1, 4):
        tile = tile + shift(take(e, (q + d) % 4).astype(BF16), "z", 2 * d).astype(F32)
    row_ids = p * B + lax.broadcasted_iota(jnp.int32, (B, NB), 0)
    col_ids = m * NB + lax.broadcasted_iota(jnp.int32, (B, NB), 1)
    tile = tile + (row_ids == col_ids).astype(F32)

    mine = from_y0(tile.reshape(2, B // 2, NB)).reshape(B, NB)
    r0, r1 = both(mine, "xhi")

    half = take(t1.reshape(2, 256, NB), c)
    d1 = both(flip(half, "xhi"), "core").reshape(NB, NB)
    w0 = inverse_factor(t0)
    low10 = mm(t1, w0, 1, 1).astype(BF16)
    block1 = d1 - mm(low10, low10, 1, 1, None)
    w1 = inverse_factor(block1)

    w0 = from_member0(w0)
    low10 = from_member0(low10)
    s0 = mm(r0, w0, 1, 1)
    lr0 = jnp.where(p >= 4, s0, 0).astype(BF16)
    lc0 = jnp.where(m >= 1, mm(w0, t0), 0).astype(BF16)
    r1 = r1 - mm(lr0, low10, 1, 1, None)
    t1 = t1 - mm(low10, lc0, 1, 0, None)
    x0 = tile - mm(lr0, lc0, 1, 0, None)

    w1 = from_member0(w1)
    s1 = mm(r1, w1, 1, 1)
    lr1 = jnp.where(p >= 8, s1, 0).astype(BF16)
    lc1 = jnp.where(m >= 2, mm(w1, t1), 0).astype(BF16)
    x1 = x0 - mm(lr1, lc1, 1, 0, None)
    solved = jnp.where(m == 0, s0, s1)
    panel = jnp.where((p < 4 * m + 4) & (col_ids > row_ids), x0, solved)
    return jnp.where((m < 2) & (p >= 4 * m), panel, x1)


def solution(mesh):
    fine = Mesh(mesh.devices.reshape(tuple(SIZES[a] for a in PIX + MEM)), PIX + MEM)
    return jax.shard_map(
        local, mesh=fine, in_specs=(P(PIX, MEM), P(PIX)), out_specs=P(PIX, MEM), check_vma=False
    )
```
